32 devices in a mesh: parts: 2 (over y), seq: 4 (over x, core), blk: 4 (over z).
Axes of the slice: x: 2, y: 2, z: 4, core: 2. Of those that a mesh axis runs over, the one named last changes fastest.
Arguments:
- queries: bfloat16 [16384, 1024], P(('parts', 'seq', 'blk')), parts along dimension 0, may hold values from -6 to 6
- keyvals: bfloat16 [2, 16384, 1024], P(None, ('parts', 'seq', 'blk')), parts along dimension 1, may hold values from -6 to 6
- key_lists: int32 [128, 12], P(('parts', 'seq', 'blk')), parts along dimension 0, may hold values from 0 to 63, as said below
- live_counts: int32 [128], P(('parts', 'seq', 'blk')), parts along dimension 0, may hold values from 4 to 12, as said below
Outputs:
- attended: bfloat16 [16384, 1024], P(('parts', 'seq', 'blk')), parts along dimension 0
The draws below stay inside these ranges and needn't reach their ends.
There are 2 independent parts, one for each index of `parts`. The reference program is written for one: setup_inputs(seed, part) draws one part's arguments, and reference() takes and returns one part's arrays. A program takes and returns all parts, laid end to end along the dimension named above; each array names one. Nothing has to cross between parts.
Inputs may be any that keep to these rules, and one draw needn't show every extreme that they name: `key_lists`: entry 0 of every list is the query block itself; the first live_counts entries of a list are distinct blocks at most 6 blocks from the query block; later entries are ignored. `live_counts`: number of used entries of each query block's key list.
All inputs are finite; a program needn't handle non-finite values.
Results may differ from the reference program's by a relative error of at most 0.0046.
Values may be sent and summed in bfloat16 or wider, within the bound.
A program may use at most 128 MiB of HBM per device.

```python
import jax
import jax.numpy as jnp
from jax import lax

HEADS = 8
HEAD_DIM = 128
BLOCK = 128
LIST = 12
REACH = 6
BLK_DEV = 4
NBLOCKS = 64


def drawn_pair(key):
    feature_width = HEADS * HEAD_DIM
    shape_three = (NBLOCKS, BLOCK, feature_width)
    query_draw = jnp.clip(jax.random.normal(jax.random.fold_in(key, 11), shape_three, jnp.float32), -6.0, 6.0)
    key_draw = jnp.clip(jax.random.normal(jax.random.fold_in(key, 12), shape_three, jnp.float32), -6.0, 6.0)
    return (query_draw.reshape(NBLOCKS * BLOCK, feature_width), key_draw.reshape(NBLOCKS * BLOCK, feature_width))


def draw_queries(key, part):
    return drawn_pair(key)[0].astype(jnp.bfloat16)


def draw_keyvals(key, part):
    key_draw = drawn_pair(key)[1]
    value_draw = jnp.clip(jax.random.normal(jax.random.fold_in(key, 15), key_draw.shape, jnp.float32), -6.0, 6.0)
    return jnp.stack([key_draw, value_draw]).astype(jnp.bfloat16)


def draw_key_lists(key, part):
    block_ids = jnp.arange(NBLOCKS, dtype=jnp.int32)
    offsets = jnp.arange(2 * REACH + 1, dtype=jnp.int32)
    candidate = block_ids[:, None] + offsets[None, :] - REACH
    in_range = (candidate >= 0) & (candidate < NBLOCKS)
    random_bits = jax.random.randint(jax.random.fold_in(key, 21), (NBLOCKS, 2 * REACH + 1), 0, 2 ** 20, dtype=jnp.int32)
    ranking = jnp.where(offsets[None, :] == REACH, 2 ** 30, jnp.where(in_range, random_bits * 64 + offsets[None, :], -1 - offsets[None, :]))
    picked = lax.top_k(ranking, LIST)[1]
    chosen = jnp.take_along_axis(candidate, picked, axis=1)
    usable = jnp.take_along_axis(in_range, picked, axis=1)
    return jnp.where(usable, chosen, block_ids[:, None]).astype(jnp.int32)


def draw_live_counts(key, part):
    block_ids = jnp.arange(NBLOCKS, dtype=jnp.int32)
    device_ids = block_ids // BLK_DEV
    heavy_device = jax.random.randint(jax.random.fold_in(key, 31), (NBLOCKS // BLK_DEV,), 0, 4, dtype=jnp.int32) == 0
    extra_range = jnp.where(heavy_device[device_ids], LIST - 4, 2)
    counts = 4 + jax.random.randint(jax.random.fold_in(key, 32), (NBLOCKS,), 0, extra_range + 1, dtype=jnp.int32)
    valid_count = jnp.minimum(block_ids, REACH) + jnp.minimum(NBLOCKS - 1 - block_ids, REACH) + 1
    counts = jnp.minimum(counts, valid_count)
    counts = jnp.where(block_ids == NBLOCKS // 2, LIST, counts)
    counts = jnp.where(block_ids == NBLOCKS // 2 + 1, 4, counts)
    return counts.astype(jnp.int32)


def setup_inputs(seed: int = 0, part: int = 0) -> dict:
    arg_keys = jax.random.split(jax.random.key(seed), 5)
    part_splits = jax.random.split(jax.random.fold_in(arg_keys[4], part), 5)
    queries = draw_queries(jax.random.fold_in(jax.random.fold_in(arg_keys[4], part), 71), part)
    keyvals = draw_keyvals(jax.random.fold_in(jax.random.fold_in(arg_keys[4], part), 71), part)
    key_lists = draw_key_lists(jax.random.fold_in(jax.random.fold_in(arg_keys[4], part), 71), part)
    live_counts = draw_live_counts(jax.random.fold_in(jax.random.fold_in(arg_keys[4], part), 71), part)
    return {"queries": queries, "keyvals": keyvals, "key_lists": key_lists, "live_counts": live_counts}


def reference(queries, keyvals, key_lists, live_counts):
    score_scale = HEAD_DIM ** -0.5
    query_blocks = queries.reshape(NBLOCKS, BLOCK, HEADS, HEAD_DIM)
    key_blocks = keyvals[0].reshape(NBLOCKS, BLOCK, HEADS, HEAD_DIM)
    value_blocks = keyvals[1].reshape(NBLOCKS, BLOCK, HEADS, HEAD_DIM)

    def attend_block(block_item):
        query_block, chosen, live_count = block_item
        key_rows = key_blocks[chosen].reshape(LIST * BLOCK, HEADS, HEAD_DIM)
        value_rows = value_blocks[chosen].reshape(LIST * BLOCK, HEADS, HEAD_DIM)
        scores = jnp.einsum("qhd,khd->hqk", query_block.astype(jnp.float32), key_rows.astype(jnp.float32)) * score_scale
        live_mask = (jnp.arange(LIST * BLOCK, dtype=jnp.int32) // BLOCK) < live_count
        scores = jnp.where(live_mask[None, None, :], scores, -jnp.inf)
        row_peak = jnp.max(scores, axis=2, keepdims=True)
        weights = jnp.exp(scores - row_peak)
        row_total = jnp.sum(weights, axis=2)
        rounded = lax.optimization_barrier(weights.astype(jnp.bfloat16))
        summed = jnp.einsum("hqk,khd->qhd", rounded.astype(jnp.float32), value_rows.astype(jnp.float32))
        result = summed / jnp.transpose(row_total)[:, :, None]
        return result.astype(jnp.bfloat16).reshape(BLOCK, HEADS * HEAD_DIM)

    attended = lax.map(attend_block, (query_blocks, key_lists, live_counts))
    return attended.reshape(NBLOCKS * BLOCK, HEADS * HEAD_DIM)
```

```python
from functools import partial

import jax
import jax.numpy as jnp
from jax import lax
from jax.experimental import pallas as pl
from jax.experimental.pallas import tpu as pltpu
from jax.sharding import PartitionSpec as P

HEADS = 8
HEAD_DIM = 128
BLOCK = 128
REACH = 6
MESH = pl.DeviceIdType.MESH


def kernel(seq_size, blk_size, lists, counts, q_hbm, kv_hbm, out, q, win, acc, peak, total, bias,
           local_sem, send_r, recv_r, send_l, recv_l):
    rows = q_hbm.shape[0]
    blocks = rows // BLOCK
    near = rows
    far = (REACH - blocks) * BLOCK
    window = 2 * (near + far) + rows
    own = near + far
    scale = HEAD_DIM ** -0.5
    here = lax.axis_index("seq") * blk_size + lax.axis_index("blk")
    last = seq_size * blk_size - 1
    has_left = here > 0
    has_right = here < last
    left = {"seq": (here - 1) // blk_size, "blk": (here - 1) % blk_size}
    right = {"seq": (here + 1) // blk_size, "blk": (here + 1) % blk_size}

    def remote(src, dst, send, recv, to, i):
        return pltpu.make_async_remote_copy(
            src_ref=src, dst_ref=dst, send_sem=send.at[i], recv_sem=recv.at[i], device_id=to, device_id_type=MESH)

    def strip(ref, start, size):
        return ref.at[:, pl.ds(start, size), :]

    to_right = [
        remote(strip(kv_hbm, rows - far, far), strip(win, own - far, far), send_r, recv_r, right, 0),
        remote(strip(kv_hbm, 0, rows - far), strip(win, far, rows - far), send_r, recv_r, right, 1),
        remote(strip(win, own - far, far), strip(win, 0, far), send_r, recv_r, right, 2),
    ]
    to_left = [
        remote(strip(kv_hbm, 0, far), strip(win, own + rows, far), send_l, recv_l, left, 0),
        remote(strip(kv_hbm, far, rows - far), strip(win, own + rows + far, rows - far), send_l, recv_l, left, 1),
        remote(strip(win, own + rows, far), strip(win, own + 2 * rows, far), send_l, recv_l, left, 2),
    ]
    fetch_q = pltpu.make_async_copy(q_hbm, q, local_sem.at[0])
    fetch_kv = pltpu.make_async_copy(kv_hbm, strip(win, own, rows), local_sem.at[1])
    fetch_q.start()
    fetch_kv.start()

    barrier = pltpu.get_barrier_semaphore()

    @pl.when(has_left)
    def _():
        pl.semaphore_signal(barrier, inc=1, device_id=left, device_id_type=MESH)

    @pl.when(has_right)
    def _():
        pl.semaphore_signal(barrier, inc=1, device_id=right, device_id_type=MESH)

    pl.semaphore_wait(barrier, has_left.astype(jnp.int32) + has_right.astype(jnp.int32))

    @pl.when(has_right)
    def _():
        to_right[0].start()

    @pl.when(has_left)
    def _():
        to_left[0].start()

    @pl.when(has_right)
    def _():
        to_right[1].start()

    @pl.when(has_left)
    def _():
        to_left[1].start()

    @pl.when(here == 0)
    def _():
        win[:, 0:own, :] = jnp.zeros((2, own, win.shape[2]), win.dtype)

    @pl.when(here == 1)
    def _():
        win[:, 0:far, :] = jnp.zeros((2, far, win.shape[2]), win.dtype)

    @pl.when(here == last)
    def _():
        win[:, own + rows:window, :] = jnp.zeros((2, own, win.shape[2]), win.dtype)

    @pl.when(here == last - 1)
    def _():
        win[:, window - far:window, :] = jnp.zeros((2, far, win.shape[2]), win.dtype)

    slot = lax.broadcasted_iota(jnp.int32, (8, window), 1) // BLOCK
    first = here * blocks - own // BLOCK
    for i in range(blocks):
        live = jnp.zeros((8, window), jnp.int32)
        for t in range(lists.shape[1]):
            listed = jnp.where(t < counts[i], lists[i, t] - first, -1)
            live = jnp.where(slot == listed, 1, live)
        bias[i] = jnp.where(live == 1, 0.0, -jnp.inf).astype(jnp.float32)

    def attend(which, start, size, opening=False, closing=False):
        def head(h, carry):
            cols = pl.ds(pl.multiple_of(h * HEAD_DIM, HEAD_DIM), HEAD_DIM)
            keys = win[0, start:start + size, cols]
            values = win[1, start:start + size, cols]
            for i in which:
                mine = slice(i * BLOCK, (i + 1) * BLOCK)
                scores = lax.dot_general(
                    q[mine, cols], keys, (((1,), (1,)), ((), ())), preferred_element_type=jnp.float32)
                scores = scores * scale + bias[i, 0:1, start:start + size]
                top = jnp.max(scores, axis=1, keepdims=True)
                if not opening:
                    before = peak[h, mine, 0:1]
                    top = jnp.maximum(top, before)
                weights = jnp.exp(scores - top)
                added = jnp.sum(weights, axis=1, keepdims=True)
                mixed = jnp.dot(weights.astype(jnp.bfloat16), values, preferred_element_type=jnp.float32)
                if not opening:
                    fade = jnp.exp(before - top)
                    added = total[h, mine, 0:1] * fade + added
                    mixed = acc[mine, cols] * fade + mixed
                if closing:
                    out[mine, cols] = (mixed / added).astype(out.dtype)
                else:
                    peak[h, mine, :] = jnp.broadcast_to(top, (BLOCK, HEAD_DIM))
                    total[h, mine, :] = jnp.broadcast_to(added, (BLOCK, HEAD_DIM))
                    acc[mine, cols] = mixed
            return carry

        lax.fori_loop(0, HEADS, head, 0)

    every = range(blocks)
    fetch_q.wait()
    fetch_kv.wait()
    attend(every, own, rows, opening=True)

    @pl.when(has_left)
    def _():
        to_right[0].wait_recv()

    @pl.when(has_left & has_right)
    def _():
        to_right[2].start()

    @pl.when(has_right)
    def _():
        to_left[0].wait_recv()

    @pl.when(has_left & has_right)
    def _():
        to_left[2].start()

    @pl.when(has_left)
    def _():
        to_right[1].wait_recv()

    attend(every, far, rows)

    @pl.when(has_right)
    def _():
        to_left[1].wait_recv()

    attend(every, own + rows, rows)

    @pl.when(here > 1)
    def _():
        to_right[2].wait_recv()

    attend([i for i in every if i * BLOCK < far], 0, far, closing=True)

    @pl.when(here < last - 1)
    def _():
        to_left[2].wait_recv()

    attend([i for i in every if i * BLOCK >= far], window - far, far, closing=True)

    @pl.when(has_right)
    def _():
        to_right[0].wait_send()
        to_right[1].wait_send()

    @pl.when(has_left)
    def _():
        to_left[0].wait_send()
        to_left[1].wait_send()

    @pl.when(has_left & has_right)
    def _():
        to_right[2].wait_send()
        to_left[2].wait_send()


def on_device(seq_size, blk_size, queries, keyvals, key_lists, live_counts):
    rows, width = queries.shape
    blocks = rows // BLOCK
    assert rows == 2 * (REACH - blocks) * BLOCK
    window = rows + 2 * REACH * BLOCK
    return pl.pallas_call(
        partial(kernel, seq_size, blk_size),
        out_shape=jax.ShapeDtypeStruct((rows, width), queries.dtype),
        in_specs=[
            pl.BlockSpec(memory_space=pltpu.SMEM),
            pl.BlockSpec(memory_space=pltpu.SMEM),
            pl.BlockSpec(memory_space=pl.ANY),
            pl.BlockSpec(memory_space=pl.ANY),
        ],
        out_specs=pl.BlockSpec(memory_space=pltpu.VMEM),
        scratch_shapes=[
            pltpu.VMEM((rows, width), jnp.bfloat16),
            pltpu.VMEM((2, window, width), jnp.bfloat16),
            pltpu.VMEM((rows, width), jnp.float32),
            pltpu.VMEM((HEADS, rows, HEAD_DIM), jnp.float32),
            pltpu.VMEM((HEADS, rows, HEAD_DIM), jnp.float32),
            pltpu.VMEM((blocks, 8, window), jnp.float32),
            pltpu.SemaphoreType.DMA((2,)),
            pltpu.SemaphoreType.DMA((3,)),
            pltpu.SemaphoreType.DMA((3,)),
            pltpu.SemaphoreType.DMA((3,)),
            pltpu.SemaphoreType.DMA((3,)),
        ],
        compiler_params=pltpu.CompilerParams(
            collective_id=0, has_side_effects=True, vmem_limit_bytes=40 * 2**20),
    )(key_lists, live_counts, queries, keyvals)


def solution(mesh):
    return jax.shard_map(
        partial(on_device, mesh.shape["seq"], mesh.shape["blk"]),
        mesh=mesh,
        in_specs=(
            P(("parts", "seq", "blk"), None),
            P(None, ("parts", "seq", "blk"), None),
            P(("parts", "seq", "blk"), None),
            P(("parts", "seq", "blk")),
        ),
        out_specs=P(("parts", "seq", "blk"), None),
        check_vma=False,
    )
```

```python
from functools import partial

import jax
import jax.numpy as jnp
from jax import lax
from jax.experimental import pallas as pl
from jax.experimental.pallas import tpu as pltpu
from jax.sharding import PartitionSpec as P

HEADS = 8
HEAD_DIM = 128
BLOCK = 128
REACH = 6
MESH = pl.DeviceIdType.MESH


def kernel(seq_size, blk_size, lists, counts, q_hbm, kv_hbm, out, q, win, held, acc, peak, total, bias,
           local_sem, send_r, recv_r, send_l, recv_l, send_h, recv_h):
    rows = q_hbm.shape[0]
    blocks = rows // BLOCK
    far_blocks = REACH - blocks
    far = far_blocks * BLOCK
    near = rows
    window = 2 * (near + far) + rows
    own = near + far
    scale = HEAD_DIM ** -0.5
    seq, blk = lax.axis_index("seq"), lax.axis_index("blk")
    here = seq * blk_size + blk
    last = seq_size * blk_size - 1
    has_left = here > 0
    has_right = here < last
    left = {"seq": (here - 1) // blk_size, "blk": (here - 1) % blk_size}
    right = {"seq": (here + 1) // blk_size, "blk": (here + 1) % blk_size}

    odd = seq % 2 == 1
    low, high = blk == 0, blk == blk_size - 1
    after = odd & (seq < seq_size - 1)
    before = jnp.logical_not(odd) & (seq > 0)
    splits_right, splits_left = after & high, before & low
    relays_right, relays_left = after & low, before & high
    corner = (after | before) & (low | high)
    across = {"seq": seq, "blk": blk_size - 1 - blk}
    over = {"seq": jnp.where(odd, seq + 1, seq - 1), "blk": blk}

    def remote(src, dst, send, recv, to):
        return pltpu.make_async_remote_copy(
            src_ref=src, dst_ref=dst, send_sem=send, recv_sem=recv, device_id=to, device_id_type=MESH)

    def strip(ref, block):
        return ref.at[:, block * BLOCK:(block + 1) * BLOCK, :]

    order_r = list(range(blocks - 1, -1, -1))
    order_l = list(range(blocks))
    to_right, to_left, to_held_r, to_held_l, held_r, held_l = [], [], [], [], [], []
    for i in range(blocks):
        for order, base, send, recv, to, direct, to_held, from_held in (
            (order_r, far_blocks, send_r, recv_r, right, to_right, to_held_r, held_r),
            (order_l, own // BLOCK + blocks, send_l, recv_l, left, to_left, to_held_l, held_l),
        ):
            mine = strip(kv_hbm, order[i])
            there = strip(win, base + order[i])
            direct.append(remote(mine, there, send.at[i], recv.at[i], to))
            if i:
                to_held.append(remote(mine, held.at[i - 1], send.at[i], recv_h.at[i - 1], across))
                from_held.append(remote(held.at[i - 1], there, send_h.at[i - 1], recv.at[i], over))
    for i in range(far_blocks):
        k = blocks + i
        b = far_blocks + order_r[i]
        to_right.append(remote(strip(win, b), strip(win, b - blocks), send_r.at[k], recv_r.at[k], right))
        b = own // BLOCK + blocks + order_l[i]
        to_left.append(remote(strip(win, b), strip(win, b + blocks), send_l.at[k], recv_l.at[k], left))

    barrier = pltpu.get_barrier_semaphore()

    @pl.when(has_left)
    def _():
        pl.semaphore_signal(barrier, inc=1, device_id=left, device_id_type=MESH)

    @pl.when(has_right)
    def _():
        pl.semaphore_signal(barrier, inc=1, device_id=right, device_id_type=MESH)

    @pl.when(corner)
    def _():
        pl.semaphore_signal(barrier, inc=1, device_id=across, device_id_type=MESH)
        pl.semaphore_signal(barrier, inc=1, device_id=over, device_id_type=MESH)

    pl.semaphore_wait(
        barrier, has_left.astype(jnp.int32) + has_right.astype(jnp.int32) + 2 * corner.astype(jnp.int32))

    for i in range(blocks):
        for exists, splits, direct, to_held in (
            (has_right, splits_right, to_right, to_held_r), (has_left, splits_left, to_left, to_held_l)):
            if i:
                pl.when(splits)(to_held[i - 1].start)
                pl.when(exists & jnp.logical_not(splits))(direct[i].start)
            else:
                pl.when(exists)(direct[i].start)

    fetch_q = pltpu.make_async_copy(q_hbm, q, local_sem.at[0])
    fetch_kv = pltpu.make_async_copy(kv_hbm, win.at[:, own:own + rows, :], local_sem.at[1])
    fetch_q.start()
    fetch_kv.start()

    @pl.when(here == 0)
    def _():
        win[:, 0:own, :] = jnp.zeros((2, own, win.shape[2]), win.dtype)

    @pl.when(here == 1)
    def _():
        win[:, 0:far, :] = jnp.zeros((2, far, win.shape[2]), win.dtype)

    @pl.when(here == last)
    def _():
        win[:, own + rows:window, :] = jnp.zeros((2, own, win.shape[2]), win.dtype)

    @pl.when(here == last - 1)
    def _():
        win[:, window - far:window, :] = jnp.zeros((2, far, win.shape[2]), win.dtype)

    slot = lax.broadcasted_iota(jnp.int32, (8, window), 1) // BLOCK
    first = here * blocks - own // BLOCK
    for i in range(blocks):
        live = jnp.zeros((8, window), jnp.int32)
        for t in range(lists.shape[1]):
            listed = jnp.where(t < counts[i], lists[i, t] - first, -1)
            live = jnp.where(slot == listed, 1, live)
        bias[i] = jnp.where(live == 1, 0.0, -jnp.inf).astype(jnp.float32)

    def attend(which, start, size, opening=False, closing=False):
        def head(h, carry):
            cols = pl.ds(pl.multiple_of(h * HEAD_DIM, HEAD_DIM), HEAD_DIM)
            keys = win[0, start:start + size, cols]
            values = win[1, start:start + size, cols]
            for i in which:
                mine = slice(i * BLOCK, (i + 1) * BLOCK)
                scores = lax.dot_general(
                    q[mine, cols], keys, (((1,), (1,)), ((), ())), preferred_element_type=jnp.float32)
                scores = scores * scale + bias[i, 0:1, start:start + size]
                top = jnp.max(scores, axis=1, keepdims=True)
                if not opening:
                    old = peak[h, mine, 0:1]
                    top = jnp.maximum(top, old)
                weights = jnp.exp(scores - top)
                added = jnp.sum(weights, axis=1, keepdims=True)
                mixed = jnp.dot(weights.astype(jnp.bfloat16), values, preferred_element_type=jnp.float32)
                if not opening:
                    fade = jnp.exp(old - top)
                    added = total[h, mine, 0:1] * fade + added
                    mixed = acc[mine, cols] * fade + mixed
                if closing:
                    out[mine, cols] = (mixed / added).astype(out.dtype)
                else:
                    peak[h, mine, :] = jnp.broadcast_to(top, (BLOCK, HEAD_DIM))
                    total[h, mine, :] = jnp.broadcast_to(added, (BLOCK, HEAD_DIM))
                    acc[mine, cols] = mixed
            return carry

        lax.fori_loop(0, HEADS, head, 0)

    every = range(blocks)
    fetch_q.wait()
    fetch_kv.wait()
    attend(every, own, rows, opening=True)

    def relay(i):
        @pl.when(relays_right)
        def _():
            to_held_r[i].wait_recv()
            held_r[i].start()

        @pl.when(relays_left)
        def _():
            to_held_l[i].wait_recv()
            held_l[i].start()

    for i in range(blocks):
        pl.when(has_left)(to_right[i].wait_recv)
        if i < far_blocks:
            pl.when(has_left & has_right)(to_right[blocks + i].start)
        pl.when(has_right)(to_left[i].wait_recv)
        if i < far_blocks:
            pl.when(has_left & has_right)(to_left[blocks + i].start)
        if i < blocks - 1:
            relay(i)

    attend(every, far, rows)
    attend(every, own + rows, rows)

    for i in range(far_blocks):
        pl.when(here > 1)(to_right[blocks + i].wait_recv)
    attend([i for i in every if i < far_blocks], 0, far, closing=True)

    for i in range(far_blocks):
        pl.when(here < last - 1)(to_left[blocks + i].wait_recv)
    attend([i for i in every if i >= far_blocks], window - far, far, closing=True)

    for i in range(blocks):
        for exists, splits, direct, to_held, relays, from_held in (
            (has_right, splits_right, to_right, to_held_r, relays_right, held_r),
            (has_left, splits_left, to_left, to_held_l, relays_left, held_l)):
            if i:
                pl.when(splits)(to_held[i - 1].wait_send)
                pl.when(exists & jnp.logical_not(splits))(direct[i].wait_send)
                pl.when(relays)(from_held[i - 1].wait_send)
            else:
                pl.when(exists)(direct[i].wait_send)
    for i in range(far_blocks):
        pl.when(has_left & has_right)(to_right[blocks + i].wait_send)
        pl.when(has_left & has_right)(to_left[blocks + i].wait_send)


def on_device(seq_size, blk_size, queries, keyvals, key_lists, live_counts):
    rows, width = queries.shape
    blocks = rows // BLOCK
    assert rows == 2 * (REACH - blocks) * BLOCK
    window = rows + 2 * REACH * BLOCK
    return pl.pallas_call(
        partial(kernel, seq_size, blk_size),
        out_shape=jax.ShapeDtypeStruct((rows, width), queries.dtype),
        in_specs=[
            pl.BlockSpec(memory_space=pltpu.SMEM),
            pl.BlockSpec(memory_space=pltpu.SMEM),
            pl.BlockSpec(memory_space=pl.ANY),
            pl.BlockSpec(memory_space=pl.ANY),
        ],
        out_specs=pl.BlockSpec(memory_space=pltpu.VMEM),
        scratch_shapes=[
            pltpu.VMEM((rows, width), jnp.bfloat16),
            pltpu.VMEM((2, window, width), jnp.bfloat16),
            pltpu.VMEM((blocks - 1, 2, BLOCK, width), jnp.bfloat16),
            pltpu.VMEM((rows, width), jnp.float32),
            pltpu.VMEM((HEADS, rows, HEAD_DIM), jnp.float32),
            pltpu.VMEM((HEADS, rows, HEAD_DIM), jnp.float32),
            pltpu.VMEM((blocks, 8, window), jnp.float32),
            pltpu.SemaphoreType.DMA((2,)),
            pltpu.SemaphoreType.DMA((REACH,)),
            pltpu.SemaphoreType.DMA((REACH,)),
            pltpu.SemaphoreType.DMA((REACH,)),
            pltpu.SemaphoreType.DMA((REACH,)),
            pltpu.SemaphoreType.DMA((blocks - 1,)),
            pltpu.SemaphoreType.DMA((blocks - 1,)),
        ],
        compiler_params=pltpu.CompilerParams(
            collective_id=0, has_side_effects=True, vmem_limit_bytes=60 * 2**20),
    )(key_lists, live_counts, queries, keyvals)


def solution(mesh):
    return jax.shard_map(
        partial(on_device, mesh.shape["seq"], mesh.shape["blk"]),
        mesh=mesh,
        in_specs=(
            P(("parts", "seq", "blk"), None),
            P(None, ("parts", "seq", "blk"), None),
            P(("parts", "seq", "blk"), None),
            P(("parts", "seq", "blk")),
        ),
        out_specs=P(("parts", "seq", "blk"), None),
        check_vma=False,
    )
```

```python
from functools import partial

import jax
import jax.numpy as jnp
from jax import lax
from jax.experimental import pallas as pl
from jax.experimental.pallas import tpu as pltpu
from jax.sharding import PartitionSpec as P

HEADS = 8
HEAD_DIM = 128
BLOCK = 128
REACH = 6
MESH = pl.DeviceIdType.MESH


def kernel(seq_size, blk_size, lists, counts, q_hbm, kv_hbm, out, q, win, held, acc, peak, total, bias,
           local_sem, send_r, recv_r, send_l, recv_l, send_h, recv_h):
    rows = q_hbm.shape[0]
    blocks = rows // BLOCK
    far_blocks = REACH - blocks
    far = far_blocks * BLOCK
    near = rows
    window = 2 * (near + far) + rows
    own = near + far
    scale = HEAD_DIM ** -0.5
    seq, blk = lax.axis_index("seq"), lax.axis_index("blk")
    here = seq * blk_size + blk
    last = seq_size * blk_size - 1
    has_left = here > 0
    has_right = here < last
    left = {"seq": (here - 1) // blk_size, "blk": (here - 1) % blk_size}
    right = {"seq": (here + 1) // blk_size, "blk": (here + 1) % blk_size}

    odd = seq % 2 == 1
    low, high = blk == 0, blk == blk_size - 1
    after = odd & (seq < seq_size - 1)
    before = jnp.logical_not(odd) & (seq > 0)
    splits_right, splits_left = after & high, before & low
    relays_right, relays_left = before & high, after & low
    corner = (after | before) & (low | high)
    across = {"seq": seq, "blk": blk_size - 1 - blk}
    over = {"seq": jnp.where(odd, seq + 1, seq - 1), "blk": blk}

    def remote(src, dst, send, recv, to):
        return pltpu.make_async_remote_copy(
            src_ref=src, dst_ref=dst, send_sem=send, recv_sem=recv, device_id=to, device_id_type=MESH)

    def strip(ref, block):
        return ref.at[:, block * BLOCK:(block + 1) * BLOCK, :]

    order_r = list(range(blocks - 1, -1, -1))
    order_l = list(range(blocks))
    to_right, to_left, to_held_r, to_held_l, held_r, held_l = [], [], [], [], [], []
    for i in range(blocks):
        for order, base, send, recv, to, direct, to_held, from_held in (
            (order_r, far_blocks, send_r, recv_r, right, to_right, to_held_r, held_r),
            (order_l, own // BLOCK + blocks, send_l, recv_l, left, to_left, to_held_l, held_l),
        ):
            mine = strip(kv_hbm, order[i])
            there = strip(win, base + order[i])
            direct.append(remote(mine, there, send.at[i], recv.at[i], to))
            if i:
                to_held.append(remote(mine, held.at[i - 1], send.at[i], recv_h.at[i - 1], over))
                from_held.append(remote(held.at[i - 1], there, send_h.at[i - 1], recv.at[i], across))
    for i in range(far_blocks):
        k = blocks + i
        b = far_blocks + order_r[i]
        to_right.append(remote(strip(win, b), strip(win, b - blocks), send_r.at[k], recv_r.at[k], right))
        b = own // BLOCK + blocks + order_l[i]
        to_left.append(remote(strip(win, b), strip(win, b + blocks), send_l.at[k], recv_l.at[k], left))

    barrier = pltpu.get_barrier_semaphore()

    @pl.when(has_left)
    def _():
        pl.semaphore_signal(barrier, inc=1, device_id=left, device_id_type=MESH)

    @pl.when(has_right)
    def _():
        pl.semaphore_signal(barrier, inc=1, device_id=right, device_id_type=MESH)

    @pl.when(corner)
    def _():
        pl.semaphore_signal(barrier, inc=1, device_id=across, device_id_type=MESH)
        pl.semaphore_signal(barrier, inc=1, device_id=over, device_id_type=MESH)

    pl.semaphore_wait(
        barrier, has_left.astype(jnp.int32) + has_right.astype(jnp.int32) + 2 * corner.astype(jnp.int32))

    for i in range(blocks):
        for exists, splits, direct, to_held in (
            (has_right, splits_right, to_right, to_held_r), (has_left, splits_left, to_left, to_held_l)):
            if i:
                pl.when(splits)(to_held[i - 1].start)
                pl.when(exists & jnp.logical_not(splits))(direct[i].start)
            else:
                pl.when(exists)(direct[i].start)

    fetch_q = pltpu.make_async_copy(q_hbm, q, local_sem.at[0])
    fetch_kv = pltpu.make_async_copy(kv_hbm, win.at[:, own:own + rows, :], local_sem.at[1])
    fetch_q.start()
    fetch_kv.start()

    @pl.when(here == 0)
    def _():
        win[:, 0:own, :] = jnp.zeros((2, own, win.shape[2]), win.dtype)

    @pl.when(here == 1)
    def _():
        win[:, 0:far, :] = jnp.zeros((2, far, win.shape[2]), win.dtype)

    @pl.when(here == last)
    def _():
        win[:, own + rows:window, :] = jnp.zeros((2, own, win.shape[2]), win.dtype)

    @pl.when(here == last - 1)
    def _():
        win[:, window - far:window, :] = jnp.zeros((2, far, win.shape[2]), win.dtype)

    slot = lax.broadcasted_iota(jnp.int32, (8, window), 1) // BLOCK
    first = here * blocks - own // BLOCK
    for i in range(blocks):
        live = jnp.zeros((8, window), jnp.int32)
        for t in range(lists.shape[1]):
            listed = jnp.where(t < counts[i], lists[i, t] - first, -1)
            live = jnp.where(slot == listed, 1, live)
        bias[i] = jnp.where(live == 1, 0.0, -jnp.inf).astype(jnp.float32)

    def attend(which, start, size, opening=False, closing=False):
        def head(h, carry):
            cols = pl.ds(pl.multiple_of(h * HEAD_DIM, HEAD_DIM), HEAD_DIM)
            keys = win[0, start:start + size, cols]
            values = win[1, start:start + size, cols]
            for i in which:
                mine = slice(i * BLOCK, (i + 1) * BLOCK)
                scores = lax.dot_general(
                    q[mine, cols], keys, (((1,), (1,)), ((), ())), preferred_element_type=jnp.float32)
                scores = scores * scale + bias[i, 0:1, start:start + size]
                top = jnp.max(scores, axis=1, keepdims=True)
                if not opening:
                    old = peak[h, mine, 0:1]
                    top = jnp.maximum(top, old)
                weights = jnp.exp(scores - top)
                added = jnp.sum(weights, axis=1, keepdims=True)
                mixed = jnp.dot(weights.astype(jnp.bfloat16), values, preferred_element_type=jnp.float32)
                if not opening:
                    fade = jnp.exp(old - top)
                    added = total[h, mine, 0:1] * fade + added
                    mixed = acc[mine, cols] * fade + mixed
                if closing:
                    out[mine, cols] = (mixed / added).astype(out.dtype)
                else:
                    peak[h, mine, :] = jnp.broadcast_to(top, (BLOCK, HEAD_DIM))
                    total[h, mine, :] = jnp.broadcast_to(added, (BLOCK, HEAD_DIM))
                    acc[mine, cols] = mixed
            return carry

        lax.fori_loop(0, HEADS, head, 0)

    every = range(blocks)
    fetch_q.wait()
    fetch_kv.wait()
    attend(every, own, rows, opening=True)

    def relay(i):
        @pl.when(relays_right)
        def _():
            to_held_r[i].wait_recv()
            held_r[i].start()

        @pl.when(relays_left)
        def _():
            to_held_l[i].wait_recv()
            held_l[i].start()

    for i in range(blocks):
        pl.when(has_left)(to_right[i].wait_recv)
        if i < far_blocks:
            pl.when(has_left & has_right)(to_right[blocks + i].start)
        pl.when(has_right)(to_left[i].wait_recv)
        if i < far_blocks:
            pl.when(has_left & has_right)(to_left[blocks + i].start)
        if i < blocks - 1:
            relay(i)

    attend(every, far, rows)
    attend(every, own + rows, rows)

    for i in range(far_blocks):
        pl.when(here > 1)(to_right[blocks + i].wait_recv)
    attend([i for i in every if i < far_blocks], 0, far, closing=True)

    for i in range(far_blocks):
        pl.when(here < last - 1)(to_left[blocks + i].wait_recv)
    attend([i for i in every if i >= far_blocks], window - far, far, closing=True)

    for i in range(blocks):
        for exists, splits, direct, to_held, relays, from_held in (
            (has_right, splits_right, to_right, to_held_r, relays_right, held_r),
            (has_left, splits_left, to_left, to_held_l, relays_left, held_l)):
            if i:
                pl.when(splits)(to_held[i - 1].wait_send)
                pl.when(exists & jnp.logical_not(splits))(direct[i].wait_send)
                pl.when(relays)(from_held[i - 1].wait_send)
            else:
                pl.when(exists)(direct[i].wait_send)
    for i in range(far_blocks):
        pl.when(has_left & has_right)(to_right[blocks + i].wait_send)
        pl.when(has_left & has_right)(to_left[blocks + i].wait_send)


def on_device(seq_size, blk_size, queries, keyvals, key_lists, live_counts):
    rows, width = queries.shape
    blocks = rows // BLOCK
    assert rows == 2 * (REACH - blocks) * BLOCK
    window = rows + 2 * REACH * BLOCK
    return pl.pallas_call(
        partial(kernel, seq_size, blk_size),
        out_shape=jax.ShapeDtypeStruct((rows, width), queries.dtype),
        in_specs=[
            pl.BlockSpec(memory_space=pltpu.SMEM),
            pl.BlockSpec(memory_space=pltpu.SMEM),
            pl.BlockSpec(memory_space=pl.ANY),
            pl.BlockSpec(memory_space=pl.ANY),
        ],
        out_specs=pl.BlockSpec(memory_space=pltpu.VMEM),
        scratch_shapes=[
            pltpu.VMEM((rows, width), jnp.bfloat16),
            pltpu.VMEM((2, window, width), jnp.bfloat16),
            pltpu.VMEM((blocks - 1, 2, BLOCK, width), jnp.bfloat16),
            pltpu.VMEM((rows, width), jnp.float32),
            pltpu.VMEM((HEADS, rows, HEAD_DIM), jnp.float32),
            pltpu.VMEM((HEADS, rows, HEAD_DIM), jnp.float32),
            pltpu.VMEM((blocks, 8, window), jnp.float32),
            pltpu.SemaphoreType.DMA((2,)),
            pltpu.SemaphoreType.DMA((REACH,)),
            pltpu.SemaphoreType.DMA((REACH,)),
            pltpu.SemaphoreType.DMA((REACH,)),
            pltpu.SemaphoreType.DMA((REACH,)),
            pltpu.SemaphoreType.DMA((blocks - 1,)),
            pltpu.SemaphoreType.DMA((blocks - 1,)),
        ],
        compiler_params=pltpu.CompilerParams(
            collective_id=0, has_side_effects=True, vmem_limit_bytes=60 * 2**20),
    )(key_lists, live_counts, queries, keyvals)


def solution(mesh):
    return jax.shard_map(
        partial(on_device, mesh.shape["seq"], mesh.shape["blk"]),
        mesh=mesh,
        in_specs=(
            P(("parts", "seq", "blk"), None),
            P(None, ("parts", "seq", "blk"), None),
            P(("parts", "seq", "blk"), None),
            P(("parts", "seq", "blk")),
        ),
        out_specs=P(("parts", "seq", "blk"), None),
        check_vma=False,
    )
```

```python
from functools import partial

import jax
import jax.numpy as jnp
from jax import lax
from jax.experimental import pallas as pl
from jax.experimental.pallas import tpu as pltpu
from jax.sharding import PartitionSpec as P

HEADS = 8
HEAD_DIM = 128
BLOCK = 128
REACH = 6
MESH = pl.DeviceIdType.MESH


def kernel(seq_size, blk_size, lists, counts, q_hbm, kv_hbm, out, q, win, held, acc, peak, total, bias,
           local_sem, send_r, recv_r, send_l, recv_l, send_h, recv_h):
    rows = q_hbm.shape[0]
    blocks = rows // BLOCK
    far_blocks = REACH - blocks
    far = far_blocks * BLOCK
    near = rows
    window = 2 * (near + far) + rows
    own = near + far
    scale = HEAD_DIM ** -0.5
    seq, blk = lax.axis_index("seq"), lax.axis_index("blk")
    here = seq * blk_size + blk
    last = seq_size * blk_size - 1
    has_left = here > 0
    has_right = here < last
    left = {"seq": (here - 1) // blk_size, "blk": (here - 1) % blk_size}
    right = {"seq": (here + 1) // blk_size, "blk": (here + 1) % blk_size}

    odd = seq % 2 == 1
    low, high = blk == 0, blk == blk_size - 1
    after = odd & (seq < seq_size - 1)
    before = jnp.logical_not(odd) & (seq > 0)
    splits_right, splits_left = after & high, before & low
    relays_right, relays_left = before & high, after & low
    corner = (after | before) & (low | high)
    across = {"seq": seq, "blk": blk_size - 1 - blk}
    over = {"seq": jnp.where(odd, seq + 1, seq - 1), "blk": blk}

    def remote(src, dst, send, recv, to):
        return pltpu.make_async_remote_copy(
            src_ref=src, dst_ref=dst, send_sem=send, recv_sem=recv, device_id=to, device_id_type=MESH)

    def strip(ref, block):
        return ref.at[:, block * BLOCK:(block + 1) * BLOCK, :]

    order_r = list(range(blocks - 1, -1, -1))
    order_l = list(range(blocks))
    to_right, to_left, to_held_r, to_held_l, held_r, held_l = [], [], [], [], [], []
    for i in range(blocks):
        for order, base, send, recv, to, direct, to_held, from_held in (
            (order_r, far_blocks, send_r, recv_r, right, to_right, to_held_r, held_r),
            (order_l, own // BLOCK + blocks, send_l, recv_l, left, to_left, to_held_l, held_l),
        ):
            mine = strip(kv_hbm, order[i])
            there = strip(win, base + order[i])
            direct.append(remote(mine, there, send.at[i], recv.at[i], to))
            if i:
                to_held.append(remote(mine, held.at[i - 1], send.at[i], recv_h.at[i - 1], over))
                from_held.append(remote(held.at[i - 1], there, send_h.at[i - 1], recv.at[i], across))
    for i in range(far_blocks):
        k = blocks + i
        b = far_blocks + order_r[i]
        to_right.append(remote(strip(win, b), strip(win, b - blocks), send_r.at[k], recv_r.at[k], right))
        b = own // BLOCK + blocks + order_l[i]
        to_left.append(remote(strip(win, b), strip(win, b + blocks), send_l.at[k], recv_l.at[k], left))

    barrier = pltpu.get_barrier_semaphore()

    @pl.when(has_left)
    def _():
        pl.semaphore_signal(barrier, inc=1, device_id=left, device_id_type=MESH)

    @pl.when(has_right)
    def _():
        pl.semaphore_signal(barrier, inc=1, device_id=right, device_id_type=MESH)

    @pl.when(corner)
    def _():
        pl.semaphore_signal(barrier, inc=1, device_id=across, device_id_type=MESH)
        pl.semaphore_signal(barrier, inc=1, device_id=over, device_id_type=MESH)

    pl.semaphore_wait(
        barrier, has_left.astype(jnp.int32) + has_right.astype(jnp.int32) + 2 * corner.astype(jnp.int32))

    for i in range(blocks):
        for exists, splits, direct, to_held in (
            (has_right, splits_right, to_right, to_held_r), (has_left, splits_left, to_left, to_held_l)):
            if i:
                pl.when(splits)(to_held[i - 1].start)
                pl.when(exists & jnp.logical_not(splits))(direct[i].start)
            else:
                pl.when(exists)(direct[i].start)

    fetch_q = pltpu.make_async_copy(q_hbm, q, local_sem.at[0])
    fetch_kv = pltpu.make_async_copy(kv_hbm, win.at[:, own:own + rows, :], local_sem.at[1])
    fetch_q.start()
    fetch_kv.start()

    @pl.when(here == 0)
    def _():
        win[:, 0:own, :] = jnp.zeros((2, own, win.shape[2]), win.dtype)

    @pl.when(here == 1)
    def _():
        win[:, 0:far, :] = jnp.zeros((2, far, win.shape[2]), win.dtype)

    @pl.when(here == last)
    def _():
        win[:, own + rows:window, :] = jnp.zeros((2, own, win.shape[2]), win.dtype)

    @pl.when(here == last - 1)
    def _():
        win[:, window - far:window, :] = jnp.zeros((2, far, win.shape[2]), win.dtype)

    slot = lax.broadcasted_iota(jnp.int32, (8, window), 1) // BLOCK
    first = here * blocks - own // BLOCK
    for i in range(blocks):
        live = jnp.zeros((8, window), jnp.int32)
        for t in range(lists.shape[1]):
            listed = jnp.where(t < counts[i], lists[i, t] - first, -1)
            live = jnp.where(slot == listed, 1, live)
        bias[i] = jnp.where(live == 1, 0.0, -jnp.inf).astype(jnp.float32)

    def attend(which, start, size, opening=False, closing=False):
        def head(h, carry):
            cols = pl.ds(pl.multiple_of(h * HEAD_DIM, HEAD_DIM), HEAD_DIM)
            keys = win[0, start:start + size, cols]
            values = win[1, start:start + size, cols]
            for i in which:
                mine = slice(i * BLOCK, (i + 1) * BLOCK)
                scores = lax.dot_general(
                    q[mine, cols], keys, (((1,), (1,)), ((), ())), preferred_element_type=jnp.float32)
                scores = scores * scale + bias[i, 0:1, start:start + size]
                top = jnp.max(scores, axis=1, keepdims=True)
                if not opening:
                    old = peak[h, mine, 0:1]
                    top = jnp.maximum(top, old)
                weights = jnp.exp(scores - top)
                added = jnp.sum(weights, axis=1, keepdims=True)
                mixed = jnp.dot(weights.astype(jnp.bfloat16), values, preferred_element_type=jnp.float32)
                if not opening:
                    fade = jnp.exp(old - top)
                    added = total[h, mine, 0:1] * fade + added
                    mixed = acc[mine, cols] * fade + mixed
                if closing:
                    out[mine, cols] = (mixed / added).astype(out.dtype)
                else:
                    peak[h, mine, :] = jnp.broadcast_to(top, (BLOCK, HEAD_DIM))
                    total[h, mine, :] = jnp.broadcast_to(added, (BLOCK, HEAD_DIM))
                    acc[mine, cols] = mixed
            return carry

        lax.fori_loop(0, HEADS, head, 0)

    every = range(blocks)
    fetch_q.wait()
    fetch_kv.wait()
    attend(every, own, rows, opening=True)

    def relay(i):
        @pl.when(relays_right)
        def _():
            to_held_r[i].wait_recv()
            held_r[i].start()

        @pl.when(relays_left)
        def _():
            to_held_l[i].wait_recv()
            held_l[i].start()

    for i in range(blocks - 1):
        relay(i)

    for i in range(blocks):
        pl.when(has_left)(to_right[i].wait_recv)
        if i < far_blocks:
            pl.when(has_left & has_right)(to_right[blocks + i].start)
        pl.when(has_right)(to_left[i].wait_recv)
        if i < far_blocks:
            pl.when(has_left & has_right)(to_left[blocks + i].start)

    attend(every, far, rows)
    attend(every, own + rows, rows)

    for i in range(far_blocks):
        pl.when(here > 1)(to_right[blocks + i].wait_recv)
    attend([i for i in every if i < far_blocks], 0, far, closing=True)

    for i in range(far_blocks):
        pl.when(here < last - 1)(to_left[blocks + i].wait_recv)
    attend([i for i in every if i >= far_blocks], window - far, far, closing=True)

    for i in range(blocks):
        for exists, splits, direct, to_held, relays, from_held in (
            (has_right, splits_right, to_right, to_held_r, relays_right, held_r),
            (has_left, splits_left, to_left, to_held_l, relays_left, held_l)):
            if i:
                pl.when(splits)(to_held[i - 1].wait_send)
                pl.when(exists & jnp.logical_not(splits))(direct[i].wait_send)
                pl.when(relays)(from_held[i - 1].wait_send)
            else:
                pl.when(exists)(direct[i].wait_send)
    for i in range(far_blocks):
        pl.when(has_left & has_right)(to_right[blocks + i].wait_send)
        pl.when(has_left & has_right)(to_left[blocks + i].wait_send)


def on_device(seq_size, blk_size, queries, keyvals, key_lists, live_counts):
    rows, width = queries.shape
    blocks = rows // BLOCK
    assert rows == 2 * (REACH - blocks) * BLOCK
    window = rows + 2 * REACH * BLOCK
    return pl.pallas_call(
        partial(kernel, seq_size, blk_size),
        out_shape=jax.ShapeDtypeStruct((rows, width), queries.dtype),
        in_specs=[
            pl.BlockSpec(memory_space=pltpu.SMEM),
            pl.BlockSpec(memory_space=pltpu.SMEM),
            pl.BlockSpec(memory_space=pl.ANY),
            pl.BlockSpec(memory_space=pl.ANY),
        ],
        out_specs=pl.BlockSpec(memory_space=pltpu.VMEM),
        scratch_shapes=[
            pltpu.VMEM((rows, width), jnp.bfloat16),
            pltpu.VMEM((2, window, width), jnp.bfloat16),
            pltpu.VMEM((blocks - 1, 2, BLOCK, width), jnp.bfloat16),
            pltpu.VMEM((rows, width), jnp.float32),
            pltpu.VMEM((HEADS, rows, HEAD_DIM), jnp.float32),
            pltpu.VMEM((HEADS, rows, HEAD_DIM), jnp.float32),
            pltpu.VMEM((blocks, 8, window), jnp.float32),
            pltpu.SemaphoreType.DMA((2,)),
            pltpu.SemaphoreType.DMA((REACH,)),
            pltpu.SemaphoreType.DMA((REACH,)),
            pltpu.SemaphoreType.DMA((REACH,)),
            pltpu.SemaphoreType.DMA((REACH,)),
            pltpu.SemaphoreType.DMA((blocks - 1,)),
            pltpu.SemaphoreType.DMA((blocks - 1,)),
        ],
        compiler_params=pltpu.CompilerParams(
            collective_id=0, has_side_effects=True, vmem_limit_bytes=60 * 2**20),
    )(key_lists, live_counts, queries, keyvals)


def solution(mesh):
    return jax.shard_map(
        partial(on_device, mesh.shape["seq"], mesh.shape["blk"]),
        mesh=mesh,
        in_specs=(
            P(("parts", "seq", "blk"), None),
            P(None, ("parts", "seq", "blk"), None),
            P(("parts", "seq", "blk"), None),
            P(("parts", "seq", "blk")),
        ),
        out_specs=P(("parts", "seq", "blk"), None),
        check_vma=False,
    )
```

```python
from functools import partial

import jax
import jax.numpy as jnp
from jax import lax
from jax.experimental import pallas as pl
from jax.experimental.pallas import tpu as pltpu
from jax.sharding import PartitionSpec as P

HEADS = 8
HEAD_DIM = 128
BLOCK = 128
REACH = 6
MESH = pl.DeviceIdType.MESH


def kernel(seq_size, blk_size, lists, counts, q_hbm, kv_hbm, out, q, win, held, acc, peak, total, bias,
           local_sem, send_r, recv_r, send_l, recv_l, send_h, recv_h):
    rows = q_hbm.shape[0]
    blocks = rows // BLOCK
    far_blocks = REACH - blocks
    far = far_blocks * BLOCK
    near = rows
    window = 2 * (near + far) + rows
    own = near + far
    scale = HEAD_DIM ** -0.5
    seq, blk = lax.axis_index("seq"), lax.axis_index("blk")
    here = seq * blk_size + blk
    last = seq_size * blk_size - 1
    has_left = here > 0
    has_right = here < last
    left = {"seq": (here - 1) // blk_size, "blk": (here - 1) % blk_size}
    right = {"seq": (here + 1) // blk_size, "blk": (here + 1) % blk_size}

    place = seq % 4 if seq_size % 4 == 0 else seq * 0 - 1
    low, high = blk == 0, blk == blk_size - 1
    splits_right, splits_left = (place == 1) & high, (place == 2) & low
    relays_right, relays_left = (place == 3) & high, (place == 0) & low
    corner = splits_right | splits_left | relays_right | relays_left
    over = {"seq": jnp.where(place < 2, seq + 2, seq - 2), "blk": blk}
    across = {"seq": jnp.where(seq % 2 == 0, seq + 1, seq - 1), "blk": blk_size - 1 - blk}

    def remote(src, dst, send, recv, to):
        return pltpu.make_async_remote_copy(
            src_ref=src, dst_ref=dst, send_sem=send, recv_sem=recv, device_id=to, device_id_type=MESH)

    def strip(ref, block):
        return ref.at[:, block * BLOCK:(block + 1) * BLOCK, :]

    order_r = list(range(blocks - 1, -1, -1))
    order_l = list(range(blocks))
    to_right, to_left, to_held_r, to_held_l, held_r, held_l = [], [], [], [], [], []
    for i in range(blocks):
        for order, base, send, recv, to, direct, to_held, from_held in (
            (order_r, far_blocks, send_r, recv_r, right, to_right, to_held_r, held_r),
            (order_l, own // BLOCK + blocks, send_l, recv_l, left, to_left, to_held_l, held_l),
        ):
            mine = strip(kv_hbm, order[i])
            there = strip(win, base + order[i])
            direct.append(remote(mine, there, send.at[i], recv.at[i], to))
            if i:
                to_held.append(remote(mine, held.at[i - 1], send.at[i], recv_h.at[i - 1], over))
                from_held.append(remote(held.at[i - 1], there, send_h.at[i - 1], recv.at[i], across))
    for i in range(far_blocks):
        k = blocks + i
        b = far_blocks + order_r[i]
        to_right.append(remote(strip(win, b), strip(win, b - blocks), send_r.at[k], recv_r.at[k], right))
        b = own // BLOCK + blocks + order_l[i]
        to_left.append(remote(strip(win, b), strip(win, b + blocks), send_l.at[k], recv_l.at[k], left))

    barrier = pltpu.get_barrier_semaphore()

    @pl.when(has_left)
    def _():
        pl.semaphore_signal(barrier, inc=1, device_id=left, device_id_type=MESH)

    @pl.when(has_right)
    def _():
        pl.semaphore_signal(barrier, inc=1, device_id=right, device_id_type=MESH)

    @pl.when(corner)
    def _():
        pl.semaphore_signal(barrier, inc=1, device_id=across, device_id_type=MESH)
        pl.semaphore_signal(barrier, inc=1, device_id=over, device_id_type=MESH)

    pl.semaphore_wait(
        barrier, has_left.astype(jnp.int32) + has_right.astype(jnp.int32) + 2 * corner.astype(jnp.int32))

    for i in range(blocks):
        for exists, splits, direct, to_held in (
            (has_right, splits_right, to_right, to_held_r), (has_left, splits_left, to_left, to_held_l)):
            if i:
                pl.when(splits)(to_held[i - 1].start)
                pl.when(exists & jnp.logical_not(splits))(direct[i].start)
            else:
                pl.when(exists)(direct[i].start)

    fetch_q = pltpu.make_async_copy(q_hbm, q, local_sem.at[0])
    fetch_kv = pltpu.make_async_copy(kv_hbm, win.at[:, own:own + rows, :], local_sem.at[1])
    fetch_q.start()
    fetch_kv.start()

    @pl.when(here == 0)
    def _():
        win[:, 0:own, :] = jnp.zeros((2, own, win.shape[2]), win.dtype)

    @pl.when(here == 1)
    def _():
        win[:, 0:far, :] = jnp.zeros((2, far, win.shape[2]), win.dtype)

    @pl.when(here == last)
    def _():
        win[:, own + rows:window, :] = jnp.zeros((2, own, win.shape[2]), win.dtype)

    @pl.when(here == last - 1)
    def _():
        win[:, window - far:window, :] = jnp.zeros((2, far, win.shape[2]), win.dtype)

    slot = lax.broadcasted_iota(jnp.int32, (8, window), 1) // BLOCK
    first = here * blocks - own // BLOCK
    for i in range(blocks):
        live = jnp.zeros((8, window), jnp.int32)
        for t in range(lists.shape[1]):
            listed = jnp.where(t < counts[i], lists[i, t] - first, -1)
            live = jnp.where(slot == listed, 1, live)
        bias[i] = jnp.where(live == 1, 0.0, -jnp.inf).astype(jnp.float32)

    def attend(which, start, size, opening=False, closing=False):
        if not which:
            return

        def head(h, carry):
            cols = pl.ds(pl.multiple_of(h * HEAD_DIM, HEAD_DIM), HEAD_DIM)
            keys = win[0, start:start + size, cols]
            values = win[1, start:start + size, cols]
            for i in which:
                mine = slice(i * BLOCK, (i + 1) * BLOCK)
                scores = lax.dot_general(
                    q[mine, cols], keys, (((1,), (1,)), ((), ())), preferred_element_type=jnp.float32)
                scores = scores * scale + bias[i, 0:1, start:start + size]
                top = jnp.max(scores, axis=1, keepdims=True)
                if not opening:
                    old = peak[h, mine, 0:1]
                    top = jnp.maximum(top, old)
                weights = jnp.exp(scores - top)
                added = jnp.sum(weights, axis=1, keepdims=True)
                mixed = jnp.dot(weights.astype(jnp.bfloat16), values, preferred_element_type=jnp.float32)
                if not opening:
                    fade = jnp.exp(old - top)
                    added = total[h, mine, 0:1] * fade + added
                    mixed = acc[mine, cols] * fade + mixed
                if closing:
                    out[mine, cols] = (mixed / added).astype(out.dtype)
                else:
                    peak[h, mine, :] = jnp.broadcast_to(top, (BLOCK, HEAD_DIM))
                    total[h, mine, :] = jnp.broadcast_to(added, (BLOCK, HEAD_DIM))
                    acc[mine, cols] = mixed
            return carry

        lax.fori_loop(0, HEADS, head, 0)

    every = range(blocks)
    fetch_q.wait()
    fetch_kv.wait()
    attend(every, own, rows, opening=True)

    def relay(i):
        @pl.when(relays_right)
        def _():
            to_held_r[i].wait_recv()
            held_r[i].start()

        @pl.when(relays_left)
        def _():
            to_held_l[i].wait_recv()
            held_l[i].start()

    for i in range(blocks - 1):
        relay(i)

    for i in range(blocks):
        pl.when(has_left)(to_right[i].wait_recv)
        if i < far_blocks:
            pl.when(has_left & has_right)(to_right[blocks + i].start)
        pl.when(has_right)(to_left[i].wait_recv)
        if i < far_blocks:
            pl.when(has_left & has_right)(to_left[blocks + i].start)

    attend(every, far, rows)
    attend(every, own + rows, rows)

    for i in range(far_blocks):
        furthest = far_blocks - 1 - i
        pl.when(here > 1)(to_right[blocks + i].wait_recv)
        attend(range(furthest), furthest * BLOCK, BLOCK)
        attend([furthest], furthest * BLOCK, BLOCK, closing=True)
        furthest = window // BLOCK - far_blocks + i
        pl.when(here < last - 1)(to_left[blocks + i].wait_recv)
        attend([blocks - far_blocks + i], furthest * BLOCK, BLOCK, closing=True)
        attend(range(blocks - far_blocks + i + 1, blocks), furthest * BLOCK, BLOCK)

    for i in range(blocks):
        for exists, splits, direct, to_held, relays, from_held in (
            (has_right, splits_right, to_right, to_held_r, relays_right, held_r),
            (has_left, splits_left, to_left, to_held_l, relays_left, held_l)):
            if i:
                pl.when(splits)(to_held[i - 1].wait_send)
                pl.when(exists & jnp.logical_not(splits))(direct[i].wait_send)
                pl.when(relays)(from_held[i - 1].wait_send)
            else:
                pl.when(exists)(direct[i].wait_send)
    for i in range(far_blocks):
        pl.when(has_left & has_right)(to_right[blocks + i].wait_send)
        pl.when(has_left & has_right)(to_left[blocks + i].wait_send)


def on_device(seq_size, blk_size, queries, keyvals, key_lists, live_counts):
    rows, width = queries.shape
    blocks = rows // BLOCK
    assert rows == 2 * (REACH - blocks) * BLOCK
    window = rows + 2 * REACH * BLOCK
    return pl.pallas_call(
        partial(kernel, seq_size, blk_size),
        out_shape=jax.ShapeDtypeStruct((rows, width), queries.dtype),
        in_specs=[
            pl.BlockSpec(memory_space=pltpu.SMEM),
            pl.BlockSpec(memory_space=pltpu.SMEM),
            pl.BlockSpec(memory_space=pl.ANY),
            pl.BlockSpec(memory_space=pl.ANY),
        ],
        out_specs=pl.BlockSpec(memory_space=pltpu.VMEM),
        scratch_shapes=[
            pltpu.VMEM((rows, width), jnp.bfloat16),
            pltpu.VMEM((2, window, width), jnp.bfloat16),
            pltpu.VMEM((blocks - 1, 2, BLOCK, width), jnp.bfloat16),
            pltpu.VMEM((rows, width), jnp.float32),
            pltpu.VMEM((HEADS, rows, HEAD_DIM), jnp.float32),
            pltpu.VMEM((HEADS, rows, HEAD_DIM), jnp.float32),
            pltpu.VMEM((blocks, 8, window), jnp.float32),
            pltpu.SemaphoreType.DMA((2,)),
            pltpu.SemaphoreType.DMA((REACH,)),
            pltpu.SemaphoreType.DMA((REACH,)),
            pltpu.SemaphoreType.DMA((REACH,)),
            pltpu.SemaphoreType.DMA((REACH,)),
            pltpu.SemaphoreType.DMA((blocks - 1,)),
            pltpu.SemaphoreType.DMA((blocks - 1,)),
        ],
        compiler_params=pltpu.CompilerParams(
            collective_id=0, has_side_effects=True, vmem_limit_bytes=60 * 2**20),
    )(key_lists, live_counts, queries, keyvals)


def solution(mesh):
    return jax.shard_map(
        partial(on_device, mesh.shape["seq"], mesh.shape["blk"]),
        mesh=mesh,
        in_specs=(
            P(("parts", "seq", "blk"), None),
            P(None, ("parts", "seq", "blk"), None),
            P(("parts", "seq", "blk"), None),
            P(("parts", "seq", "blk")),
        ),
        out_specs=P(("parts", "seq", "blk"), None),
        check_vma=False,
    )
```

```python
from functools import partial

import jax
import jax.numpy as jnp
from jax import lax
from jax.experimental import pallas as pl
from jax.experimental.pallas import tpu as pltpu
from jax.sharding import PartitionSpec as P

HEADS = 8
HEAD_DIM = 128
BLOCK = 128
REACH = 6
MESH = pl.DeviceIdType.MESH


def kernel(seq_size, blk_size, lists, counts, q_hbm, kv_hbm, out, q, win, held, acc, peak, total, bias,
           local_sem, send_r, recv_r, send_l, recv_l, send_h, recv_h):
    rows = q_hbm.shape[0]
    blocks = rows // BLOCK
    far_blocks = REACH - blocks
    far = far_blocks * BLOCK
    near = rows
    window = 2 * (near + far) + rows
    own = near + far
    scale = HEAD_DIM ** -0.5
    seq, blk = lax.axis_index("seq"), lax.axis_index("blk")
    here = seq * blk_size + blk
    last = seq_size * blk_size - 1
    has_left = here > 0
    has_right = here < last
    left = {"seq": (here - 1) // blk_size, "blk": (here - 1) % blk_size}
    right = {"seq": (here + 1) // blk_size, "blk": (here + 1) % blk_size}

    odd = seq % 2 == 1
    low, high = blk == 0, blk == blk_size - 1
    after = odd & (seq < seq_size - 1)
    before = jnp.logical_not(odd) & (seq > 0)
    splits_right, splits_left = after & high, before & low
    relays_right, relays_left = before & high, after & low
    corner = (after | before) & (low | high)
    across = {"seq": seq, "blk": blk_size - 1 - blk}
    over = {"seq": jnp.where(odd, seq + 1, seq - 1), "blk": blk}

    def remote(src, dst, send, recv, to):
        return pltpu.make_async_remote_copy(
            src_ref=src, dst_ref=dst, send_sem=send, recv_sem=recv, device_id=to, device_id_type=MESH)

    def strip(ref, block):
        return ref.at[:, block * BLOCK:(block + 1) * BLOCK, :]

    order_r = list(range(blocks - 1, -1, -1))
    order_l = list(range(blocks))
    to_right, to_left, to_held_r, to_held_l, held_r, held_l = [], [], [], [], [], []
    for i in range(blocks):
        for order, base, send, recv, to, direct, to_held, from_held in (
            (order_r, far_blocks, send_r, recv_r, right, to_right, to_held_r, held_r),
            (order_l, own // BLOCK + blocks, send_l, recv_l, left, to_left, to_held_l, held_l),
        ):
            mine = strip(kv_hbm, order[i])
            there = strip(win, base + order[i])
            direct.append(remote(mine, there, send.at[i], recv.at[i], to))
            if i:
                to_held.append(remote(mine, held.at[i - 1], send.at[i], recv_h.at[i - 1], over))
                from_held.append(remote(held.at[i - 1], there, send_h.at[i - 1], recv.at[i], across))
    for i in range(far_blocks):
        k = blocks + i
        b = far_blocks + order_r[i]
        to_right.append(remote(strip(win, b), strip(win, b - blocks), send_r.at[k], recv_r.at[k], right))
        b = own // BLOCK + blocks + order_l[i]
        to_left.append(remote(strip(win, b), strip(win, b + blocks), send_l.at[k], recv_l.at[k], left))

    barrier = pltpu.get_barrier_semaphore()

    @pl.when(has_left)
    def _():
        pl.semaphore_signal(barrier, inc=1, device_id=left, device_id_type=MESH)

    @pl.when(has_right)
    def _():
        pl.semaphore_signal(barrier, inc=1, device_id=right, device_id_type=MESH)

    @pl.when(corner)
    def _():
        pl.semaphore_signal(barrier, inc=1, device_id=across, device_id_type=MESH)
        pl.semaphore_signal(barrier, inc=1, device_id=over, device_id_type=MESH)

    pl.semaphore_wait(
        barrier, has_left.astype(jnp.int32) + has_right.astype(jnp.int32) + 2 * corner.astype(jnp.int32))

    for i in range(blocks):
        for exists, splits, direct, to_held in (
            (has_right, splits_right, to_right, to_held_r), (has_left, splits_left, to_left, to_held_l)):
            if i:
                pl.when(splits)(to_held[i - 1].start)
                pl.when(exists & jnp.logical_not(splits))(direct[i].start)
            else:
                pl.when(exists)(direct[i].start)

    fetch_q = pltpu.make_async_copy(q_hbm, q, local_sem.at[0])
    fetch_kv = pltpu.make_async_copy(kv_hbm, win.at[:, own:own + rows, :], local_sem.at[1])
    fetch_q.start()
    fetch_kv.start()

    @pl.when(here == 0)
    def _():
        win[:, 0:own, :] = jnp.zeros((2, own, win.shape[2]), win.dtype)

    @pl.when(here == 1)
    def _():
        win[:, 0:far, :] = jnp.zeros((2, far, win.shape[2]), win.dtype)

    @pl.when(here == last)
    def _():
        win[:, own + rows:window, :] = jnp.zeros((2, own, win.shape[2]), win.dtype)

    @pl.when(here == last - 1)
    def _():
        win[:, window - far:window, :] = jnp.zeros((2, far, win.shape[2]), win.dtype)

    slot = lax.broadcasted_iota(jnp.int32, (8, window), 1) // BLOCK
    first = here * blocks - own // BLOCK
    for i in range(blocks):
        live = jnp.zeros((8, window), jnp.int32)
        for t in range(lists.shape[1]):
            listed = jnp.where(t < counts[i], lists[i, t] - first, -1)
            live = jnp.where(slot == listed, 1, live)
        bias[i] = jnp.where(live == 1, 0.0, -jnp.inf).astype(jnp.float32)

    def attend(which, start, size, opening=False, closing=False):
        if not which:
            return

        def head(h, carry):
            cols = pl.ds(pl.multiple_of(h * HEAD_DIM, HEAD_DIM), HEAD_DIM)
            keys = win[0, start:start + size, cols]
            values = win[1, start:start + size, cols]
            for i in which:
                mine = slice(i * BLOCK, (i + 1) * BLOCK)
                scores = lax.dot_general(
                    q[mine, cols], keys, (((1,), (1,)), ((), ())), preferred_element_type=jnp.float32)
                scores = scores * scale + bias[i, 0:1, start:start + size]
                top = jnp.max(scores, axis=1, keepdims=True)
                if not opening:
                    old = peak[h, mine, 0:1]
                    top = jnp.maximum(top, old)
                weights = jnp.exp(scores - top)
                added = jnp.sum(weights, axis=1, keepdims=True)
                mixed = jnp.dot(weights.astype(jnp.bfloat16), values, preferred_element_type=jnp.float32)
                if not opening:
                    fade = jnp.exp(old - top)
                    added = total[h, mine, 0:1] * fade + added
                    mixed = acc[mine, cols] * fade + mixed
                if closing:
                    out[mine, cols] = (mixed / added).astype(out.dtype)
                else:
                    peak[h, mine, :] = jnp.broadcast_to(top, (BLOCK, HEAD_DIM))
                    total[h, mine, :] = jnp.broadcast_to(added, (BLOCK, HEAD_DIM))
                    acc[mine, cols] = mixed
            return carry

        lax.fori_loop(0, HEADS, head, 0)

    every = range(blocks)
    fetch_q.wait()
    fetch_kv.wait()
    attend(every, own, rows, opening=True)

    def relay(i):
        @pl.when(relays_right)
        def _():
            to_held_r[i].wait_recv()
            held_r[i].start()

        @pl.when(relays_left)
        def _():
            to_held_l[i].wait_recv()
            held_l[i].start()

    for i in range(blocks - 1):
        relay(i)

    for i in range(blocks):
        pl.when(has_left)(to_right[i].wait_recv)
        if i < far_blocks:
            pl.when(has_left & has_right)(to_right[blocks + i].start)
        pl.when(has_right)(to_left[i].wait_recv)
        if i < far_blocks:
            pl.when(has_left & has_right)(to_left[blocks + i].start)

    attend(every, far, rows)
    attend(every, own + rows, rows)

    for i in range(far_blocks):
        furthest = far_blocks - 1 - i
        pl.when(here > 1)(to_right[blocks + i].wait_recv)
        attend(range(furthest), furthest * BLOCK, BLOCK)
        attend([furthest], furthest * BLOCK, BLOCK, closing=True)
        furthest = window // BLOCK - far_blocks + i
        pl.when(here < last - 1)(to_left[blocks + i].wait_recv)
        attend([blocks - far_blocks + i], furthest * BLOCK, BLOCK, closing=True)
        attend(range(blocks - far_blocks + i + 1, blocks), furthest * BLOCK, BLOCK)

    for i in range(blocks):
        for exists, splits, direct, to_held, relays, from_held in (
            (has_right, splits_right, to_right, to_held_r, relays_right, held_r),
            (has_left, splits_left, to_left, to_held_l, relays_left, held_l)):
            if i:
                pl.when(splits)(to_held[i - 1].wait_send)
                pl.when(exists & jnp.logical_not(splits))(direct[i].wait_send)
                pl.when(relays)(from_held[i - 1].wait_send)
            else:
                pl.when(exists)(direct[i].wait_send)
    for i in range(far_blocks):
        pl.when(has_left & has_right)(to_right[blocks + i].wait_send)
        pl.when(has_left & has_right)(to_left[blocks + i].wait_send)


def on_device(seq_size, blk_size, queries, keyvals, key_lists, live_counts):
    rows, width = queries.shape
    blocks = rows // BLOCK
    assert rows == 2 * (REACH - blocks) * BLOCK
    window = rows + 2 * REACH * BLOCK
    return pl.pallas_call(
        partial(kernel, seq_size, blk_size),
        out_shape=jax.ShapeDtypeStruct((rows, width), queries.dtype),
        in_specs=[
            pl.BlockSpec(memory_space=pltpu.SMEM),
            pl.BlockSpec(memory_space=pltpu.SMEM),
            pl.BlockSpec(memory_space=pl.ANY),
            pl.BlockSpec(memory_space=pl.ANY),
        ],
        out_specs=pl.BlockSpec(memory_space=pltpu.VMEM),
        scratch_shapes=[
            pltpu.VMEM((rows, width), jnp.bfloat16),
            pltpu.VMEM((2, window, width), jnp.bfloat16),
            pltpu.VMEM((blocks - 1, 2, BLOCK, width), jnp.bfloat16),
            pltpu.VMEM((rows, width), jnp.float32),
            pltpu.VMEM((HEADS, rows, HEAD_DIM), jnp.float32),
            pltpu.VMEM((HEADS, rows, HEAD_DIM), jnp.float32),
            pltpu.VMEM((blocks, 8, window), jnp.float32),
            pltpu.SemaphoreType.DMA((2,)),
            pltpu.SemaphoreType.DMA((REACH,)),
            pltpu.SemaphoreType.DMA((REACH,)),
            pltpu.SemaphoreType.DMA((REACH,)),
            pltpu.SemaphoreType.DMA((REACH,)),
            pltpu.SemaphoreType.DMA((blocks - 1,)),
            pltpu.SemaphoreType.DMA((blocks - 1,)),
        ],
        compiler_params=pltpu.CompilerParams(
            collective_id=0, has_side_effects=True, vmem_limit_bytes=60 * 2**20),
    )(key_lists, live_counts, queries, keyvals)


def solution(mesh):
    return jax.shard_map(
        partial(on_device, mesh.shape["seq"], mesh.shape["blk"]),
        mesh=mesh,
        in_specs=(
            P(("parts", "seq", "blk"), None),
            P(None, ("parts", "seq", "blk"), None),
            P(("parts", "seq", "blk"), None),
            P(("parts", "seq", "blk")),
        ),
        out_specs=P(("parts", "seq", "blk"), None),
        check_vma=False,
    )
```
